32 devices in a mesh: od: 16 (over z, x, core), lk: 2 (over y).
Axes of the slice: x: 2, y: 2, z: 4, core: 2. Of those that a mesh axis runs over, the one named last changes fastest.
Arguments:
- factor: bfloat16 [131072, 256], P('od'), may hold values from -6 to 6
- prior_mean: bfloat16 [131072], P('od'), may hold values from -192 to 192
- counts: float32 [16384], P(('od', 'lk')), may hold values from -8192 to 8192
- noise_std: float32 [16384], P(('od', 'lk')), may hold values from 1638.4 to 16384
- owner_ids: int32 [128, 8], P('od'), may hold values from 0 to 15, all different within a row; in each aligned block of 8 rows (0 to 7, 8 to 15, ...) at most 8 rows name the same one
- local_ids: int32 [128, 8], P('od'), may hold values from 0 to 63
- ecmp: int32 [128, 8], P('od'), may hold values from 1 to 4
- route_share: bfloat16 [128, 8, 128, 128], P('od'), may hold values from 0 to 1
Outputs:
- new_factor: float32 [131072, 256], P(('od', 'lk'))
- correction: float32 [131072], P(('od', 'lk'))
The draws below stay inside these ranges and needn't reach their ends.
Inputs may be any that keep to these rules, and one draw needn't show every extreme that they name: `owner_ids`: each tile names 8 different owners; the 8 tiles of one aligned group name any owner at most 8 times, and some group names some owner exactly 8 times.
All inputs are finite; a program needn't handle non-finite values.
Results may differ from the reference program's by a relative error of at most 0.0003.
Values may be sent and summed in bfloat16 or wider, within the bound.
A program may use at most 128 MiB of HBM per device.

```python
import math
import jax
import jax.numpy as jnp
import numpy as np
from jax import lax

R = 256
BLK = 128
TL = 128
NB = 8
ODS = 131072
BLK_DEV = 64
LINKS = 16384
TILES = 128
TILES_GRP = 8
SLOTS = 8
N_OD = 16


def touch_ends(result, key, low, largest):
    longest = result.shape.index(max(result.shape))
    spots = []
    for shift in (0, 1):
        where = [jax.random.randint(jax.random.fold_in(key, axis), (), 0, length) for axis, length in enumerate(result.shape)]
        where[longest] = (where[longest] + shift) % result.shape[longest]
        spots.append(tuple(where))
    return result.at[spots[0]].set(low).at[spots[1]].set(largest)


def level_of(stream_key, extent, cuts, least, high):
    level, own = 1.0, jax.random.fold_in(stream_key, 6)
    for axis_at, parts in cuts:
        heights = jnp.exp(jax.random.uniform(jax.random.fold_in(own, axis_at), (parts,), jnp.float32, least / len(cuts), high / len(cuts)))
        level = level * jnp.repeat(heights, extent[axis_at] // parts).reshape([-1 if axis == axis_at else 1 for axis in range(len(extent))])
    return level


def deal_out(stream_key, own, number, rows, count, top, limit, lean):
    order = jax.random.permutation(stream_key, count)
    heavy_load, ordinary = portions_of(count, rows * top, limit, lean, True), portions_of(count, rows * top, limit, lean, False)
    places = jnp.arange(count)

    def named(tallies, turn):
        used = int((tallies > 0).sum())
        fixed = max(1, used // 4)
        moved = fixed + (places - fixed + turn * (used - fixed)) % max(1, count - fixed)
        return jnp.zeros((count,), jnp.int32).at[order[jnp.where(places < fixed, places, moved)]].set(jnp.asarray(tallies, jnp.int32))

    tallies = jnp.where(number % 4 == 0, named(heavy_load, number // 4), named(ordinary, number - number // 4 - 1))
    mixed = jax.random.permutation(jax.random.fold_in(own, 3), count)
    donor, taker = mixed[0:count // 2 * 2:2], mixed[1:count // 2 * 2:2]
    margin = jnp.minimum(tallies[donor] - 1, limit - tallies[taker]) // 2
    margin = jnp.where((donor == order[0]) | (taker == order[0]) | (tallies[taker] == 0), 0, jnp.maximum(margin, 0))
    moved = jax.random.randint(jax.random.fold_in(own, 4), (count // 2,), 0, 1 << 20) % (margin + 1)
    tallies = tallies.at[donor].add(-moved).at[taker].add(moved)
    members = jnp.searchsorted(jnp.cumsum(tallies), jnp.arange(rows * top), side="right").astype(jnp.int32)
    listing = members.reshape(top, rows).T
    listing = listing[jax.random.permutation(jax.random.fold_in(own, 1), rows)]
    turn = jax.random.randint(jax.random.fold_in(own, 2), (rows, 1), 0, top)
    return jnp.take_along_axis(listing, (jnp.arange(top)[None, :] + turn) % top, axis=1)


def portions_of(number_of, total, reach, skew, full):
    loads = [(1 << 20) // math.isqrt(grade ** skew) + 1 for grade in range(1, number_of + 1)]
    largest = reach if full else min(reach, max(-(-total // number_of), total * loads[0] // sum(loads)))
    least = 1 if total - largest >= number_of - 1 else 0
    given, spare = [largest] + [least] * (number_of - 1), total - largest - least * (number_of - 1)
    while spare > 0:
        candidates = [i for i in range(1, number_of) if given[i] < largest] or [i for i in range(1, number_of) if given[i] < reach]
        mass, left = sum([loads[i] for i in candidates]), spare
        for i in candidates:
            more = min(reach - given[i], max(1, left * loads[i] // mass), spare)
            given[i] = given[i] + more
            spare = spare - more
    return np.array(given)


def noise(key, extent, scale, most, cuts=(), kind=jnp.bfloat16):
    gain = level_of(key, extent, cuts, -0.22, 0.18) if cuts else 1.0
    drawn = jax.random.normal(key, extent, jnp.float32) * scale * gain
    return jnp.minimum(jnp.maximum(drawn, -most), most).astype(kind)


def setup_inputs(seed: int = 0) -> dict:
    key_list = jax.random.split(jax.random.key(seed), 9)
    factor = noise(key_list[0], (ODS, R), 1.0, 6.0, ((0, 16),))
    prior_mean = noise(key_list[1], (ODS,), 30.0, 192.0, ((0, 16),))
    counts = noise(key_list[2], (LINKS,), (30 * (NB * BLK * 2.5) ** 0.5), 8192.0, ((0, 32),), jnp.float32)
    noise_std = jnp.clip(jnp.exp(math.log(16384.0) - 2.3025851 * jax.random.uniform(key_list[3], (LINKS,), jnp.float32) ** level_of(key_list[3], (LINKS,), ((0, 32),), -0.2, 0.2)), 1638.4, 16384.0)
    owner_ids_keys = jax.random.split(jax.random.fold_in(key_list[4], 1), TILES // TILES_GRP)
    owner_ids_turns = jax.random.permutation(jax.random.fold_in(key_list[4], 3), TILES // TILES_GRP)
    owner_ids = jax.vmap(lambda own, number: deal_out(jax.random.fold_in(key_list[4], 2), own, number, TILES_GRP, N_OD, NB, SLOTS, 1))(owner_ids_keys, owner_ids_turns).reshape((TILES, NB))
    local_ids = touch_ends(jax.random.randint(key_list[5], (TILES, NB), 0, BLK_DEV), jax.random.fold_in(key_list[5], 1), 0, BLK_DEV - 1).astype(jnp.int32)
    ecmp = touch_ends(jax.random.randint(key_list[6], (TILES, NB), 1, 5), jax.random.fold_in(key_list[6], 1), 1, 4).astype(jnp.int32)
    route_share = jnp.clip(1.0 * jax.random.uniform(key_list[7], (TILES, NB, TL, BLK), jnp.float32) ** level_of(key_list[7], (TILES, NB, TL, BLK), ((0, 16),), -0.2, 0.2), 0.0, 1.0).astype(jnp.bfloat16)
    return dict(factor=factor, prior_mean=prior_mean, counts=counts, noise_std=noise_std, owner_ids=owner_ids, local_ids=local_ids, ecmp=ecmp, route_share=route_share)


def reference(factor, prior_mean, counts, noise_std, owner_ids, local_ids, ecmp, route_share):
    blocks = owner_ids * BLK_DEV + local_ids
    fac_blocks = factor.reshape(-1, BLK, R)
    mean_blocks = prior_mean.reshape(-1, BLK)

    def one_group(pieces):
        block_ids, shares, multiples = pieces
        gathered = fac_blocks[block_ids].astype(jnp.float32)
        means = mean_blocks[block_ids].astype(jnp.float32)
        wide_share = shares.astype(jnp.float32)
        scaled = multiples.astype(jnp.float32)
        linked_grp = jnp.sum(jnp.einsum('tkab,tkbc->tkac', wide_share, gathered, precision=lax.Precision.HIGHEST) * scaled[:, :, None, None], axis=1)
        predicted_grp = jnp.sum(jnp.einsum('tkab,tkb->tka', wide_share, means, precision=lax.Precision.HIGHEST) * scaled[:, :, None], axis=1)
        return (linked_grp, predicted_grp)
    linked, predicted = lax.map(one_group, (blocks.reshape(-1, TILES_GRP, NB), route_share.reshape(-1, TILES_GRP, NB, TL, BLK), ecmp.reshape(-1, TILES_GRP, NB)))
    linked = linked.reshape(LINKS, R)
    predicted = predicted.reshape(LINKS)
    whitened = linked / noise_std[:, None]
    innovation = (counts - predicted) / noise_std
    gram = jnp.dot(whitened.T.astype(jnp.float32), whitened.astype(jnp.float32), precision=lax.Precision.HIGHEST, preferred_element_type=jnp.float32)
    projected = jnp.dot(whitened.T.astype(jnp.float32), innovation.astype(jnp.float32), precision=lax.Precision.HIGHEST, preferred_element_type=jnp.float32)
    identity = jnp.eye(R, dtype=jnp.float32)
    lower = jnp.linalg.cholesky(identity + gram)
    inverse = jax.scipy.linalg.solve_triangular(lower, identity, lower=True)
    inner = jnp.dot(inverse.astype(jnp.float32), projected.astype(jnp.float32), precision=lax.Precision.HIGHEST, preferred_element_type=jnp.float32)
    gain_vector = jnp.dot(inverse.T.astype(jnp.float32), inner.astype(jnp.float32), precision=lax.Precision.HIGHEST, preferred_element_type=jnp.float32)
    factor_wide = factor.astype(jnp.float32)
    new_factor = jnp.dot(factor_wide.astype(jnp.float32), inverse.T.astype(jnp.float32), precision=lax.Precision.HIGHEST, preferred_element_type=jnp.float32)
    correction = jnp.dot(factor_wide.astype(jnp.float32), gain_vector.astype(jnp.float32), precision=lax.Precision.HIGHEST, preferred_element_type=jnp.float32)
    return (new_factor, correction)
```

```python
import functools

import jax
import jax.numpy as jnp
from jax import lax
from jax.experimental import pallas as pl
from jax.experimental.pallas import tpu as pltpu
from jax.sharding import PartitionSpec as P

MESH = pl.DeviceIdType.MESH
HIGHEST = lax.Precision.HIGHEST
VMEM = pltpu.VMEM


def dot(a, b, contract, precision=None):
    return lax.dot_general(
        a, b, (contract, ((), ())), precision=precision, preferred_element_type=jnp.float32
    )


def link_kernel(
    n, tiles, nb, owner_ref, local_ref, ecmp_ref, mean_ref, counts_ref, std_ref,
    fac_ref, route_hbm, out_ref,
    ask, got_ask, ask_smem, send_f, got_f, send_m, got_m, route, white,
    ask_send, ask_recv, f_send, f_recv, m_send, m_recv, local_sem, route_sem,
):
    me = lax.axis_index("od")
    first = lax.axis_index("lk") * tiles
    rank = fac_ref.shape[2]

    load_route = pltpu.make_async_copy(route_hbm.at[pl.ds(first, tiles)], route, route_sem)
    load_route.start()

    barrier = pltpu.get_barrier_semaphore()

    def greet(step, carry):
        peer = lax.rem(me + step, n)
        pl.semaphore_signal(barrier, inc=1, device_id={"od": peer}, device_id_type=MESH)
        return carry

    lax.fori_loop(1, n, greet, 0)

    owner_iota = lax.broadcasted_iota(jnp.int32, ask.shape, 0)
    lane = lax.broadcasted_iota(jnp.int32, ask.shape, 2)
    table = jnp.zeros(ask.shape, jnp.int32)
    for t in range(tiles):
        for k in range(nb):
            hit = (owner_iota == owner_ref[first + t, k]) & (lane == t)
            table = jnp.where(hit, local_ref[first + t, k], table)
    ask[...] = table
    send_m[...] = jnp.zeros_like(send_m)
    pl.semaphore_wait(barrier, n - 1)

    def push(src, dst, send_sem, recv_sem, at, peer):
        return pltpu.make_async_remote_copy(
            src_ref=src, dst_ref=dst.at[at], send_sem=send_sem.at[peer],
            recv_sem=recv_sem.at[at], device_id={"od": peer}, device_id_type=MESH,
        )

    def ask_peer(step, carry):
        peer = lax.rem(me + step, n)
        push(ask.at[peer], got_ask, ask_send, ask_recv, me, peer).start()
        return carry

    lax.fori_loop(1, n, ask_peer, 0)
    got_ask[me] = ask[me]

    def await_ask(step, carry):
        peer = lax.rem(me + step, n)
        push(ask.at[peer], got_ask, ask_send, ask_recv, peer, peer).wait_recv()
        return carry

    lax.fori_loop(1, n, await_ask, 0)
    to_smem = pltpu.make_async_copy(got_ask, ask_smem, local_sem)
    to_smem.start()
    to_smem.wait()

    def serve(step, carry):
        peer = lax.rem(me + step, n)
        for t in range(tiles):
            index = ask_smem[peer, 0, t]
            send_f[peer, t] = fac_ref[index]
            send_m[peer, t:t + 1] = mean_ref[index]
        push(send_m.at[peer], got_m, m_send, m_recv, me, peer).start()
        push(send_f.at[peer], got_f, f_send, f_recv, me, peer).start()
        return carry

    lax.fori_loop(1, n, serve, 0)
    own_m = jnp.zeros((1,) + send_m.shape[1:], jnp.float32)
    got_m[me] = own_m[0]
    for t in range(tiles):
        index = ask_smem[me, 0, t]
        got_f[me, t] = fac_ref[index]
        got_m[me, t:t + 1] = mean_ref[index]
    spread = [jnp.broadcast_to(std_ref[t:t + 1, :], (128, 128)).T for t in range(tiles)]
    load_route.wait()

    def await_blocks(step, carry):
        peer = lax.rem(me + step, n)
        push(send_m.at[peer], got_m, m_send, m_recv, peer, peer).wait_recv()
        push(send_f.at[peer], got_f, f_send, f_recv, peer, peer).wait_recv()
        return carry

    lax.fori_loop(1, n, await_blocks, 0)

    gram = jnp.zeros((rank, rank), jnp.float32)
    projected = jnp.zeros((8, rank), jnp.float32)
    for t in range(tiles):
        linked = jnp.zeros((128, rank), jnp.float32)
        predicted = jnp.zeros((8, 128), jnp.float32)
        for k in range(nb):
            owner = owner_ref[first + t, k]
            times = ecmp_ref[first + t, k].astype(jnp.float32)
            share = route[t, k]
            linked += times * dot(share, got_f[owner, t], ((1,), (0,)))
            predicted += times * dot(got_m[owner].astype(jnp.bfloat16), share, ((1,), (1,)))
        noise = jnp.concatenate([spread[t]] * (rank // 128), axis=1)
        whitened = linked / noise
        innovation = (counts_ref[t:t + 1, :] - predicted[t:t + 1, :]) / std_ref[t:t + 1, :]
        white[t * 128:(t + 1) * 128, :] = whitened
        projected += dot(
            jnp.broadcast_to(innovation, (8, 128)), whitened, ((1,), (0,)), HIGHEST
        )
    whole = white[...]
    gram = dot(whole.T, whole, ((1,), (0,)), HIGHEST)
    row = lax.broadcasted_iota(jnp.int32, (8, rank), 0)
    column = lax.broadcasted_iota(jnp.int32, (8, rank), 1)
    head = gram[0:8, :]
    head = jnp.where((row == 0) & (column > 0), projected, head)
    head = jnp.where((row == 1) & (column == rank - 1), projected[:, 0:1], head)
    out_ref[...] = gram
    out_ref[0:8, :] = head

    def drain(step, carry):
        peer = lax.rem(me + step, n)
        push(ask.at[peer], got_ask, ask_send, ask_recv, me, peer).wait_send()
        push(send_m.at[peer], got_m, m_send, m_recv, me, peer).wait_send()
        push(send_f.at[peer], got_f, f_send, f_recv, me, peer).wait_send()
        return carry

    lax.fori_loop(1, n, drain, 0)


def sum_kernel(n_od, n_lk, in_ref, out_ref, got, full, send1, recv1, send2, recv2):
    n = n_od * n_lk
    me = lax.axis_index("od") * n_lk + lax.axis_index("lk")

    def place(step):
        peer = lax.rem(me + step, n)
        return peer, {"od": peer // n_lk, "lk": lax.rem(peer, n_lk)}

    barrier = pltpu.get_barrier_semaphore()

    def greet(step, carry):
        _, where = place(step)
        pl.semaphore_signal(barrier, inc=1, device_id=where, device_id_type=MESH)
        return carry

    lax.fori_loop(1, n, greet, 0)
    pl.semaphore_wait(barrier, n - 1)

    def scatter(step, at_me):
        peer, where = place(step)
        at = me if at_me else peer
        return pltpu.make_async_remote_copy(
            src_ref=in_ref.at[peer], dst_ref=got.at[at], send_sem=send1.at[peer],
            recv_sem=recv1.at[at], device_id=where, device_id_type=MESH,
        )

    def gather(step, at_me):
        peer, where = place(step)
        at = me if at_me else peer
        return pltpu.make_async_remote_copy(
            src_ref=full.at[me], dst_ref=full.at[at], send_sem=send2.at[peer],
            recv_sem=recv2.at[at], device_id=where, device_id_type=MESH,
        )

    def every(action):
        def body(step, carry):
            action(step)
            return carry

        lax.fori_loop(1, n, body, 0)

    every(lambda step: scatter(step, True).start())
    got[me] = in_ref[me]
    every(lambda step: scatter(step, False).wait_recv())
    full[me] = jnp.sum(got[...], axis=0)
    every(lambda step: gather(step, True).start())
    every(lambda step: gather(step, False).wait_recv())
    out_ref[...] = full[...]
    every(lambda step: scatter(step, True).wait_send())
    every(lambda step: gather(step, True).wait_send())


@jax.jit
def inverse_factor(a):
    size = a.shape[0]
    lane = lax.broadcasted_iota(jnp.int32, (1, size), 1)
    sub = lax.broadcasted_iota(jnp.int32, (8, size), 0)
    lanes = lax.broadcasted_iota(jnp.int32, (8, size), 1)
    groups = [a[8 * g:8 * g + 8, :] for g in range(size // 8)]
    for j in range(size):
        at, offset = j // 8, j % 8
        here = lane == j
        row = groups[at][offset:offset + 1, :]
        scaled = jnp.where(here, 1.0, row) / row[:, j:j + 1]
        for g in range(at, size // 8):
            if g == at and offset == 7:
                continue
            old = groups[g]
            new = jnp.where(here, 0.0, old) - old[:, j:j + 1] * scaled
            groups[g] = jnp.where(sub > offset, new, old) if g == at else new
    done = []
    for g, rows in enumerate(groups):
        diagonal = lanes == sub + 8 * g
        pivot = jnp.sum(jnp.where(diagonal, rows, 0.0), axis=1, keepdims=True)
        unit = jnp.where(diagonal, 1.0, jnp.where(lanes < sub + 8 * g, rows, 0.0))
        done.append(unit * lax.rsqrt(pivot))
    return jnp.concatenate(done, axis=0)


def update_kernel(start_ref, gram_ref, fac_ref, new_ref, corr_ref, high, low, gain):
    rank = gram_ref.shape[0]
    half = rank // 2

    @pl.when(pl.program_id(0) == 0)
    def _():
        lane = lax.broadcasted_iota(jnp.int32, (half, half), 1)
        sub = lax.broadcasted_iota(jnp.int32, (half, half), 0)

        def symmetric(block):
            upper = block.T
            return jnp.where(sub >= lane, block, upper) + jnp.where(sub == lane, 1.0, 0.0)

        a11 = symmetric(gram_ref[:half, :half])
        a21 = gram_ref[half:, :half]
        w1 = inverse_factor(a11)
        l21 = dot(a21, w1, ((1,), (1,)), HIGHEST)
        a22 = symmetric(gram_ref[half:, half:]) - dot(l21, l21, ((1,), (1,)), HIGHEST)
        w2 = inverse_factor(a22)
        w21 = -dot(w2, dot(l21, w1, ((1,), (0,)), HIGHEST), ((1,), (0,)), HIGHEST)
        inverse = jnp.concatenate(
            [jnp.concatenate([w1, jnp.zeros((half, half), jnp.float32)], axis=1),
             jnp.concatenate([w21, w2], axis=1)], axis=0,
        )
        lane = lax.broadcasted_iota(jnp.int32, (8, rank), 1)
        projected = jnp.broadcast_to(gram_ref[0:1, :], (8, rank))
        projected = jnp.where(lane == 0, gram_ref[1:2, rank - 1:rank], projected)
        inner = dot(projected, inverse, ((1,), (1,)), HIGHEST)
        vector = dot(inner, inverse, ((1,), (0,)), HIGHEST)
        top = vector.astype(jnp.bfloat16)
        rest = vector - top.astype(jnp.float32)
        middle = rest.astype(jnp.bfloat16)
        last = (rest - middle.astype(jnp.float32)).astype(jnp.bfloat16)
        gain[...] = jnp.concatenate([top, middle, last], axis=0)
        turned = inverse.T
        upper = turned.astype(jnp.bfloat16)
        high[...] = upper
        low[...] = (turned - upper.astype(jnp.float32)).astype(jnp.bfloat16)

    rows = fac_ref[...]
    new_ref[...] = dot(rows, high[...], ((1,), (0,))) + dot(rows, low[...], ((1,), (0,)))
    parts = dot(gain[...], rows, ((1,), (1,)))
    corr_ref[0] = parts[0:1] + parts[8:9] + parts[16:17]


def per_device(factor, prior_mean, counts, noise_std, owner_ids, local_ids, ecmp, route_share):
    n_od, n_lk = lax.axis_size("od"), lax.axis_size("lk")
    group_tiles, nb = owner_ids.shape
    tiles = group_tiles // n_lk
    link_rows, block_rows = route_share.shape[2:]
    rank = factor.shape[1]
    blocks = factor.shape[0] // block_rows
    vmem = pl.BlockSpec(memory_space=VMEM)
    smem = pl.BlockSpec(memory_space=pltpu.SMEM)
    dma = pltpu.SemaphoreType.DMA

    packed = pl.pallas_call(
        functools.partial(link_kernel, n_od, tiles, nb),
        out_shape=jax.ShapeDtypeStruct((rank, rank), jnp.float32),
        in_specs=[smem, smem, smem, vmem, vmem, vmem, vmem, pl.BlockSpec(memory_space=pl.ANY)],
        out_specs=vmem,
        scratch_shapes=[
            VMEM((n_od, 8, 128), jnp.int32),
            VMEM((n_od, 8, 128), jnp.int32),
            pltpu.SMEM((n_od, 8, 128), jnp.int32),
            VMEM((n_od, tiles, block_rows, rank), jnp.bfloat16),
            VMEM((n_od, tiles, block_rows, rank), jnp.bfloat16),
            VMEM((n_od, 8, block_rows), jnp.float32),
            VMEM((n_od, 8, block_rows), jnp.float32),
            VMEM((tiles, nb, link_rows, block_rows), jnp.bfloat16),
            VMEM((tiles * link_rows, rank), jnp.float32),
        ] + [dma((n_od,))] * 6 + [dma, dma],
        compiler_params=pltpu.CompilerParams(
            collective_id=0, has_side_effects=True, vmem_limit_bytes=56 * 1024 * 1024
        ),
        name="links",
    )(
        owner_ids, local_ids, ecmp,
        prior_mean.astype(jnp.float32).reshape(blocks, 1, block_rows),
        counts.reshape(tiles, link_rows), noise_std.reshape(tiles, link_rows),
        factor.reshape(blocks, block_rows, rank), route_share,
    )

    n_all = n_od * n_lk
    slab = (n_all, rank // n_all, rank)
    summed = pl.pallas_call(
        functools.partial(sum_kernel, n_od, n_lk),
        out_shape=jax.ShapeDtypeStruct(slab, jnp.float32),
        in_specs=[vmem],
        out_specs=vmem,
        scratch_shapes=[VMEM(slab, jnp.float32), VMEM(slab, jnp.float32)]
        + [dma((n_all,))] * 4,
        compiler_params=pltpu.CompilerParams(
            collective_id=1, has_side_effects=True, vmem_limit_bytes=32 * 1024 * 1024
        ),
        name="sums",
    )(packed.reshape(slab)).reshape(rank, rank)

    own_rows = factor.shape[0] // n_lk
    step_rows = min(512, own_rows)
    steps = own_rows // step_rows
    start = (lax.axis_index("lk") * steps).astype(jnp.int32).reshape(1)
    new_factor, correction = pl.pallas_call(
        update_kernel,
        out_shape=(
            jax.ShapeDtypeStruct((own_rows, rank), jnp.float32),
            jax.ShapeDtypeStruct((steps, 1, step_rows), jnp.float32),
        ),
        grid_spec=pltpu.PrefetchScalarGridSpec(
            num_scalar_prefetch=1,
            grid=(steps,),
            in_specs=[
                pl.BlockSpec((rank, rank), lambda i, start: (0, 0)),
                pl.BlockSpec((step_rows, rank), lambda i, start: (start[0] + i, 0)),
            ],
            out_specs=[
                pl.BlockSpec((step_rows, rank), lambda i, start: (i, 0)),
                pl.BlockSpec((1, 1, step_rows), lambda i, start: (i, 0, 0)),
            ],
            scratch_shapes=[
                VMEM((rank, rank), jnp.bfloat16),
                VMEM((rank, rank), jnp.bfloat16),
                VMEM((24, rank), jnp.bfloat16),
            ],
        ),
        compiler_params=pltpu.CompilerParams(vmem_limit_bytes=32 * 1024 * 1024),
        name="update",
    )(start, summed, factor)
    return (new_factor, correction.reshape(-1))


def solution(mesh):
    in_specs = (
        P("od", None),
        P("od"),
        P(("od", "lk")),
        P(("od", "lk")),
        P("od", None),
        P("od", None),
        P("od", None),
        P("od", None, None, None),
    )
    out_specs = (P(("od", "lk"), None), P(("od", "lk")))
    return jax.shard_map(
        per_device, mesh=mesh, in_specs=in_specs, out_specs=out_specs, check_vma=False
    )
```

```python
import functools

import jax
import jax.numpy as jnp
from jax import lax
from jax.experimental import pallas as pl
from jax.experimental.pallas import tpu as pltpu
from jax.sharding import PartitionSpec as P

MESH = pl.DeviceIdType.MESH
HIGHEST = lax.Precision.HIGHEST
VMEM = pltpu.VMEM


def dot(a, b, contract, precision=None):
    return lax.dot_general(
        a, b, (contract, ((), ())), precision=precision, preferred_element_type=jnp.float32
    )


def split(a):
    high = a.astype(jnp.bfloat16)
    return high, (a - high.astype(jnp.float32)).astype(jnp.bfloat16)


def link_kernel(
    n, n_lk, tiles, nb, owner_ref, local_ref, ecmp_ref, mean_ref, counts_ref, std_ref,
    fac_ref, route_hbm, out_ref,
    ask, got_ask, ask_smem, send_f, got_f, send_m, got_m, route, linked, predicted,
    sums, got_s, full,
    ask_send, ask_recv, f_send, f_recv, m_send, m_recv, s_send, s_recv, t_send, t_recv,
    local_sem, route_sem,
):
    me, my_lk = lax.axis_index("od"), lax.axis_index("lk")
    first = my_lk * tiles
    rank = fac_ref.shape[2]
    n_all = n * n_lk
    me_all = me * n_lk + my_lk
    half = n // 2

    load_route = pltpu.make_async_copy(route_hbm.at[pl.ds(first, tiles)], route, route_sem)
    load_route.start()

    barrier = pltpu.get_barrier_semaphore()

    def loop(start, stop, action):
        def body(step, carry):
            action(step)
            return carry

        lax.fori_loop(start, stop, body, 0)

    def place(index):
        return {"od": index // n_lk, "lk": lax.rem(index, n_lk)}

    def greet(step):
        where = place(lax.rem(me_all + step, n_all))
        pl.semaphore_signal(barrier, inc=1, device_id=where, device_id_type=MESH)

    loop(1, n_all, greet)

    owner_iota = lax.broadcasted_iota(jnp.int32, ask.shape, 0)
    lane = lax.broadcasted_iota(jnp.int32, ask.shape, 2)
    table = jnp.zeros(ask.shape, jnp.int32)
    for t in range(tiles):
        for k in range(nb):
            hit = (owner_iota == owner_ref[first + t, k]) & (lane == t)
            table = jnp.where(hit, local_ref[first + t, k], table)
    ask[...] = table
    send_m[...] = jnp.zeros_like(send_m)
    linked[...] = jnp.zeros_like(linked)
    predicted[...] = jnp.zeros_like(predicted)
    pl.semaphore_wait(barrier, n_all - 1)

    def push(src, dst, send_sem, recv_sem, at, peer):
        return pltpu.make_async_remote_copy(
            src_ref=src, dst_ref=dst.at[at], send_sem=send_sem.at[peer],
            recv_sem=recv_sem.at[at], device_id={"od": peer}, device_id_type=MESH,
        )

    def far(step):
        return (1 - me // half) * half + lax.rem(me + step, half)

    def near(step):
        return (me // half) * half + lax.rem(me + step, half)

    def others(action, far_first):
        if far_first:
            loop(0, half, lambda step: action(far(step)))
        loop(1, half, lambda step: action(near(step)))
        if not far_first:
            loop(0, half, lambda step: action(far(step)))

    others(lambda peer: push(ask.at[peer], got_ask, ask_send, ask_recv, me, peer).start(), True)
    got_ask[me] = ask[me]
    others(
        lambda peer: push(ask.at[peer], got_ask, ask_send, ask_recv, peer, peer).wait_recv(), False
    )
    to_smem = pltpu.make_async_copy(got_ask, ask_smem, local_sem)
    to_smem.start()
    to_smem.wait()

    def serve(peer):
        for t in range(tiles):
            index = ask_smem[peer, 0, t]
            send_f[peer, t] = fac_ref[index]
            send_m[peer, t:t + 1] = mean_ref[index]
        push(send_m.at[peer], got_m, m_send, m_recv, me, peer).start()
        push(send_f.at[peer], got_f, f_send, f_recv, me, peer).start()

    others(serve, True)
    got_m[me] = jnp.zeros(send_m.shape[1:], jnp.float32)
    for t in range(tiles):
        index = ask_smem[me, 0, t]
        got_f[me, t] = fac_ref[index]
        got_m[me, t:t + 1] = mean_ref[index]
    spread = [jnp.broadcast_to(std_ref[t:t + 1, :], (128, 128)).T for t in range(tiles)]
    load_route.wait()

    def use(owner):
        means = got_m[owner].astype(jnp.bfloat16)
        for t in range(tiles):
            slot, times = 0, 0
            for k in range(nb):
                named = owner_ref[first + t, k] == owner
                slot = jnp.where(named, k, slot)
                times = jnp.where(named, ecmp_ref[first + t, k], times)
            times = times.astype(jnp.float32)
            share = route[t, slot]
            linked[t] += times * dot(share, got_f[owner, t], ((1,), (0,)))
            predicted[t] += times * dot(means, share, ((1,), (1,)))

    def arrive(peer):
        push(send_m.at[peer], got_m, m_send, m_recv, peer, peer).wait_recv()
        push(send_f.at[peer], got_f, f_send, f_recv, peer, peer).wait_recv()
        use(peer)

    use(me)
    others(arrive, False)

    whole, innovation = [], []
    for t in range(tiles):
        whole.append(linked[t] / jnp.concatenate([spread[t]] * (rank // 128), axis=1))
        innovation.append(
            (counts_ref[t:t + 1, :] - predicted[t, t:t + 1, :]) / std_ref[t:t + 1, :]
        )
    high, low = split(jnp.concatenate(whole, axis=0))
    in_high, in_low = split(jnp.broadcast_to(
        jnp.concatenate(innovation, axis=1), (8, tiles * 128)
    ))
    cross = dot(high, low, ((0,), (0,)))
    gram = dot(high, high, ((0,), (0,))) + (cross + cross.T)
    projected = dot(in_high, high, ((1,), (0,))) + (
        dot(in_low, high, ((1,), (0,))) + dot(in_high, low, ((1,), (0,)))
    )
    mid = rank // 2
    row = lax.broadcasted_iota(jnp.int32, (mid, mid), 0)
    column = lax.broadcasted_iota(jnp.int32, (mid, mid), 1)
    last = gram[mid:, mid:]
    slabs = mid // 8
    sums[0:slabs, :, :mid] = gram[mid:, :mid].reshape(slabs, 8, mid)
    sums[0:slabs, :, mid:] = jnp.where(row >= column, gram[:mid, :mid], last).reshape(
        slabs, 8, mid
    )
    diagonal = jnp.sum(jnp.where(row == column, last, 0.0), axis=0, keepdims=True)
    diagonal = jnp.concatenate([diagonal, diagonal], axis=1)
    eight = lax.broadcasted_iota(jnp.int32, (8, rank), 0)
    sums[slabs] = jnp.where(eight == 0, projected, diagonal)

    stride = n_all // slabs
    summer = (me % stride == 0) | ((me == 1) & (my_lk == 0))
    mine = jnp.where(me % stride == 0, (me // stride) * n_lk + my_lk, slabs)

    def home(i):
        last_one = i // slabs
        return (
            (1 - last_one) * (i // n_lk) * stride + last_one,
            (1 - last_one) * lax.rem(i, n_lk),
        )

    def to_home(i):
        od, lk = home(i)
        return pltpu.make_async_remote_copy(
            src_ref=sums.at[i], dst_ref=got_s.at[me_all], send_sem=s_send.at[i],
            recv_sem=s_recv.at[me_all], device_id={"od": od, "lk": lk}, device_id_type=MESH,
        )

    def not_mine(action):
        def body(i):
            od, lk = home(i)

            @pl.when((od != me) | (lk != my_lk))
            def _():
                action(i)

        loop(0, slabs + 1, body)

    def from_home(step, i):
        peer = lax.rem(me_all + step, n_all)
        return pltpu.make_async_remote_copy(
            src_ref=full.at[i], dst_ref=full.at[i], send_sem=t_send.at[step],
            recv_sem=t_recv.at[i], device_id=place(peer), device_id_type=MESH,
        )

    def await_part(step):
        peer = lax.rem(me_all + step, n_all)
        pltpu.make_async_remote_copy(
            src_ref=sums.at[0], dst_ref=got_s.at[peer], send_sem=s_send.at[0],
            recv_sem=s_recv.at[peer], device_id=place(peer), device_id_type=MESH,
        ).wait_recv()

    not_mine(lambda i: to_home(i).start())

    @pl.when(summer)
    def _():
        got_s[me_all] = sums[mine]
        loop(1, n_all, await_part)
        full[mine] = jnp.sum(got_s[...], axis=0)
        loop(1, n_all, lambda step: from_home(step, mine).start())

    not_mine(lambda i: from_home(1, i).wait_recv())
    out_ref[...] = full[...]

    def drain(peer):
        push(ask.at[peer], got_ask, ask_send, ask_recv, me, peer).wait_send()
        push(send_m.at[peer], got_m, m_send, m_recv, me, peer).wait_send()
        push(send_f.at[peer], got_f, f_send, f_recv, me, peer).wait_send()

    others(drain, True)
    not_mine(lambda i: to_home(i).wait_send())

    @pl.when(summer)
    def _():
        loop(1, n_all, lambda step: from_home(step, mine).wait_send())


@jax.jit
def inverse_factor(a):
    size = a.shape[0]
    lane = lax.broadcasted_iota(jnp.int32, (1, size), 1)
    sub = lax.broadcasted_iota(jnp.int32, (8, size), 0)
    lanes = lax.broadcasted_iota(jnp.int32, (8, size), 1)
    groups = [a[8 * g:8 * g + 8, :] for g in range(size // 8)]
    for j in range(size):
        at, offset = j // 8, j % 8
        here = lane == j
        row = groups[at][offset:offset + 1, :]
        scaled = jnp.where(here, 1.0, row) / row[:, j:j + 1]
        for g in range(at, size // 8):
            if g == at and offset == 7:
                continue
            old = groups[g]
            new = jnp.where(here, 0.0, old) - old[:, j:j + 1] * scaled
            groups[g] = jnp.where(sub > offset, new, old) if g == at else new
    done = []
    for g, rows in enumerate(groups):
        diagonal = lanes == sub + 8 * g
        pivot = jnp.sum(jnp.where(diagonal, rows, 0.0), axis=1, keepdims=True)
        unit = jnp.where(diagonal, 1.0, jnp.where(lanes < sub + 8 * g, rows, 0.0))
        done.append(unit * lax.rsqrt(pivot))
    return jnp.concatenate(done, axis=0)


def update_kernel(start_ref, gram_ref, fac_ref, new_ref, corr_ref, high, low, gain):
    rank = gram_ref.shape[2]
    half = rank // 2
    slabs = half // 8

    @pl.when(pl.program_id(0) == 0)
    def _():
        lane = lax.broadcasted_iota(jnp.int32, (half, half), 1)
        sub = lax.broadcasted_iota(jnp.int32, (half, half), 0)

        packed = gram_ref[0:slabs].reshape(half, rank)
        a21, both = packed[:, :half], packed[:, half:]
        turned = both.T
        extra = gram_ref[slabs]
        a11 = jnp.where(sub >= lane, both, turned) + jnp.where(sub == lane, 1.0, 0.0)
        a22 = jnp.where(sub < lane, both, turned)
        a22 = jnp.where(sub == lane, 1.0 + extra[1:2, :half], a22)
        w1 = inverse_factor(a11)
        l21 = dot(a21, w1, ((1,), (1,)), HIGHEST)
        a22 = a22 - dot(l21, l21, ((1,), (1,)), HIGHEST)
        w2 = inverse_factor(a22)
        w21 = -dot(w2, dot(l21, w1, ((1,), (0,)), HIGHEST), ((1,), (0,)), HIGHEST)
        inverse = jnp.concatenate(
            [jnp.concatenate([w1, jnp.zeros((half, half), jnp.float32)], axis=1),
             jnp.concatenate([w21, w2], axis=1)], axis=0,
        )
        projected = jnp.broadcast_to(extra[0:1, :], (8, rank))
        inner = dot(projected, inverse, ((1,), (1,)), HIGHEST)
        vector = dot(inner, inverse, ((1,), (0,)), HIGHEST)
        top = vector.astype(jnp.bfloat16)
        rest = vector - top.astype(jnp.float32)
        middle = rest.astype(jnp.bfloat16)
        last = (rest - middle.astype(jnp.float32)).astype(jnp.bfloat16)
        gain[...] = jnp.concatenate([top, middle, last], axis=0)
        turned = inverse.T
        upper = turned.astype(jnp.bfloat16)
        high[...] = upper
        low[...] = (turned - upper.astype(jnp.float32)).astype(jnp.bfloat16)

    rows = fac_ref[...]
    new_ref[...] = dot(rows, high[...], ((1,), (0,))) + dot(rows, low[...], ((1,), (0,)))
    parts = dot(gain[...], rows, ((1,), (1,)))
    corr_ref[0] = parts[0:1] + parts[8:9] + parts[16:17]


def per_device(factor, prior_mean, counts, noise_std, owner_ids, local_ids, ecmp, route_share):
    n_od, n_lk = lax.axis_size("od"), lax.axis_size("lk")
    group_tiles, nb = owner_ids.shape
    tiles = group_tiles // n_lk
    link_rows, block_rows = route_share.shape[2:]
    rank = factor.shape[1]
    blocks = factor.shape[0] // block_rows
    vmem = pl.BlockSpec(memory_space=VMEM)
    smem = pl.BlockSpec(memory_space=pltpu.SMEM)
    dma = pltpu.SemaphoreType.DMA

    n_all = n_od * n_lk
    slabs = rank // 16 + 1
    slab = (slabs, 8, rank)
    summed = pl.pallas_call(
        functools.partial(link_kernel, n_od, n_lk, tiles, nb),
        out_shape=jax.ShapeDtypeStruct(slab, jnp.float32),
        in_specs=[smem, smem, smem, vmem, vmem, vmem, vmem, pl.BlockSpec(memory_space=pl.ANY)],
        out_specs=vmem,
        scratch_shapes=[
            VMEM((n_od, 8, 128), jnp.int32),
            VMEM((n_od, 8, 128), jnp.int32),
            pltpu.SMEM((n_od, 8, 128), jnp.int32),
            VMEM((n_od, tiles, block_rows, rank), jnp.bfloat16),
            VMEM((n_od, tiles, block_rows, rank), jnp.bfloat16),
            VMEM((n_od, 8, block_rows), jnp.float32),
            VMEM((n_od, 8, block_rows), jnp.float32),
            VMEM((tiles, nb, link_rows, block_rows), jnp.bfloat16),
            VMEM((tiles, link_rows, rank), jnp.float32),
            VMEM((tiles, 8, link_rows), jnp.float32),
            VMEM(slab, jnp.float32),
            VMEM((n_all, 8, rank), jnp.float32),
            VMEM(slab, jnp.float32),
        ] + [dma((n_od,))] * 6 + [dma((slabs,)), dma((n_all,)), dma((n_all,)), dma((slabs,))]
        + [dma, dma],
        compiler_params=pltpu.CompilerParams(
            collective_id=0, has_side_effects=True, vmem_limit_bytes=56 * 1024 * 1024
        ),
        name="links",
    )(
        owner_ids, local_ids, ecmp,
        prior_mean.astype(jnp.float32).reshape(blocks, 1, block_rows),
        counts.reshape(tiles, link_rows), noise_std.reshape(tiles, link_rows),
        factor.reshape(blocks, block_rows, rank), route_share,
    )

    own_rows = factor.shape[0] // n_lk
    step_rows = min(512, own_rows)
    steps = own_rows // step_rows
    start = (lax.axis_index("lk") * steps).astype(jnp.int32).reshape(1)
    new_factor, correction = pl.pallas_call(
        update_kernel,
        out_shape=(
            jax.ShapeDtypeStruct((own_rows, rank), jnp.float32),
            jax.ShapeDtypeStruct((steps, 1, step_rows), jnp.float32),
        ),
        grid_spec=pltpu.PrefetchScalarGridSpec(
            num_scalar_prefetch=1,
            grid=(steps,),
            in_specs=[
                pl.BlockSpec(slab, lambda i, start: (0, 0, 0)),
                pl.BlockSpec((step_rows, rank), lambda i, start: (start[0] + i, 0)),
            ],
            out_specs=[
                pl.BlockSpec((step_rows, rank), lambda i, start: (i, 0)),
                pl.BlockSpec((1, 1, step_rows), lambda i, start: (i, 0, 0)),
            ],
            scratch_shapes=[
                VMEM((rank, rank), jnp.bfloat16),
                VMEM((rank, rank), jnp.bfloat16),
                VMEM((24, rank), jnp.bfloat16),
            ],
        ),
        compiler_params=pltpu.CompilerParams(vmem_limit_bytes=32 * 1024 * 1024),
        name="update",
    )(start, summed, factor)
    return (new_factor, correction.reshape(-1))


def solution(mesh):
    in_specs = (
        P("od", None),
        P("od"),
        P(("od", "lk")),
        P(("od", "lk")),
        P("od", None),
        P("od", None),
        P("od", None),
        P("od", None, None, None),
    )
    out_specs = (P(("od", "lk"), None), P(("od", "lk")))
    return jax.shard_map(
        per_device, mesh=mesh, in_specs=in_specs, out_specs=out_specs, check_vma=False
    )
```

```python
import functools

import jax
import jax.numpy as jnp
from jax import lax
from jax.experimental import pallas as pl
from jax.experimental.pallas import tpu as pltpu
from jax.sharding import PartitionSpec as P

MESH = pl.DeviceIdType.MESH
HIGHEST = lax.Precision.HIGHEST
VMEM = pltpu.VMEM


def dot(a, b, contract, precision=None):
    return lax.dot_general(
        a, b, (contract, ((), ())), precision=precision, preferred_element_type=jnp.float32
    )


def split(a):
    high = a.astype(jnp.bfloat16)
    return high, (a - high.astype(jnp.float32)).astype(jnp.bfloat16)


def link_kernel(
    n, n_lk, tiles, nb, owner_ref, local_ref, ecmp_ref, mean_ref, counts_ref, std_ref,
    fac_ref, route_hbm, out_ref,
    ask, got_ask, ask_smem, send_f, got_f, send_m, got_m, route, linked, predicted,
    sums, got_s, full,
    ask_send, ask_recv, f_send, f_recv, m_send, m_recv, s_send, s_recv, t_send, t_recv,
    local_sem, route_sem,
):
    me, my_lk = lax.axis_index("od"), lax.axis_index("lk")
    first = my_lk * tiles
    rank = fac_ref.shape[2]
    n_all = n * n_lk
    me_all = me * n_lk + my_lk
    half = n // 2

    load_route = pltpu.make_async_copy(route_hbm.at[pl.ds(first, tiles)], route, route_sem)
    load_route.start()

    barrier = pltpu.get_barrier_semaphore()

    def loop(start, stop, action):
        def body(step, carry):
            action(step)
            return carry

        lax.fori_loop(start, stop, body, 0)

    def place(index):
        return {"od": index // n_lk, "lk": lax.rem(index, n_lk)}

    def greet(step):
        where = place(lax.rem(me_all + step, n_all))
        pl.semaphore_signal(barrier, inc=1, device_id=where, device_id_type=MESH)

    loop(1, n_all, greet)

    owner_iota = lax.broadcasted_iota(jnp.int32, ask.shape, 0)
    lane = lax.broadcasted_iota(jnp.int32, ask.shape, 2)
    table = jnp.zeros(ask.shape, jnp.int32)
    for t in range(tiles):
        for k in range(nb):
            hit = (owner_iota == owner_ref[first + t, k]) & (lane == t)
            table = jnp.where(hit, local_ref[first + t, k], table)
    ask[...] = table
    send_m[...] = jnp.zeros_like(send_m)
    linked[...] = jnp.zeros_like(linked)
    predicted[...] = jnp.zeros_like(predicted)
    pl.semaphore_wait(barrier, n_all - 1)

    def push(src, dst, send_sem, recv_sem, at, peer):
        return pltpu.make_async_remote_copy(
            src_ref=src, dst_ref=dst.at[at], send_sem=send_sem.at[peer],
            recv_sem=recv_sem.at[at], device_id={"od": peer}, device_id_type=MESH,
        )

    def far(step):
        return (1 - me // half) * half + lax.rem(me + step, half)

    def near(step):
        return (me // half) * half + lax.rem(me + step, half)

    def others(action, far_first):
        if far_first:
            loop(0, half, lambda step: action(far(step)))
        loop(1, half, lambda step: action(near(step)))
        if not far_first:
            loop(0, half, lambda step: action(far(step)))

    others(lambda peer: push(ask.at[peer], got_ask, ask_send, ask_recv, me, peer).start(), True)
    got_ask[me] = ask[me]
    others(
        lambda peer: push(ask.at[peer], got_ask, ask_send, ask_recv, peer, peer).wait_recv(), False
    )
    to_smem = pltpu.make_async_copy(got_ask, ask_smem, local_sem)
    to_smem.start()
    to_smem.wait()

    def serve(peer):
        for t in range(tiles):
            index = ask_smem[peer, 0, t]
            send_f[peer, t] = fac_ref[index]
            send_m[peer, t:t + 1] = mean_ref[index]
        push(send_m.at[peer], got_m, m_send, m_recv, me, peer).start()
        push(send_f.at[peer], got_f, f_send, f_recv, me, peer).start()

    loop(1, n, lambda step: serve(lax.rem(me + step, n)))
    got_m[me] = jnp.zeros(send_m.shape[1:], jnp.float32)
    for t in range(tiles):
        index = ask_smem[me, 0, t]
        got_f[me, t] = fac_ref[index]
        got_m[me, t:t + 1] = mean_ref[index]
    spread = [jnp.broadcast_to(std_ref[t:t + 1, :], (128, 128)).T for t in range(tiles)]
    load_route.wait()

    def use(owner):
        means = got_m[owner].astype(jnp.bfloat16)
        for t in range(tiles):
            slot, times = 0, 0
            for k in range(nb):
                named = owner_ref[first + t, k] == owner
                slot = jnp.where(named, k, slot)
                times = jnp.where(named, ecmp_ref[first + t, k], times)
            times = times.astype(jnp.float32)
            share = route[t, slot]
            linked[t] += times * dot(share, got_f[owner, t], ((1,), (0,)))
            predicted[t] += times * dot(means, share, ((1,), (1,)))

    def arrive(peer):
        push(send_m.at[peer], got_m, m_send, m_recv, peer, peer).wait_recv()
        push(send_f.at[peer], got_f, f_send, f_recv, peer, peer).wait_recv()
        use(peer)

    use(me)
    others(arrive, False)

    whole, innovation = [], []
    for t in range(tiles):
        whole.append(linked[t] / jnp.concatenate([spread[t]] * (rank // 128), axis=1))
        innovation.append(
            (counts_ref[t:t + 1, :] - predicted[t, t:t + 1, :]) / std_ref[t:t + 1, :]
        )
    high, low = split(jnp.concatenate(whole, axis=0))
    in_high, in_low = split(jnp.broadcast_to(
        jnp.concatenate(innovation, axis=1), (8, tiles * 128)
    ))
    cross = dot(high, low, ((0,), (0,)))
    gram = dot(high, high, ((0,), (0,))) + (cross + cross.T)
    projected = dot(in_high, high, ((1,), (0,))) + (
        dot(in_low, high, ((1,), (0,))) + dot(in_high, low, ((1,), (0,)))
    )
    mid = rank // 2
    row = lax.broadcasted_iota(jnp.int32, (mid, mid), 0)
    column = lax.broadcasted_iota(jnp.int32, (mid, mid), 1)
    last = gram[mid:, mid:]
    slabs = mid // 8
    sums[0:slabs, :, :mid] = gram[mid:, :mid].reshape(slabs, 8, mid)
    sums[0:slabs, :, mid:] = jnp.where(row >= column, gram[:mid, :mid], last).reshape(
        slabs, 8, mid
    )
    diagonal = jnp.sum(jnp.where(row == column, last, 0.0), axis=0, keepdims=True)
    diagonal = jnp.concatenate([diagonal, diagonal], axis=1)
    eight = lax.broadcasted_iota(jnp.int32, (8, rank), 0)
    sums[slabs] = jnp.where(eight == 0, projected, diagonal)

    stride = n_all // slabs
    summer = (me % stride == 0) | ((me == 1) & (my_lk == 0))
    mine = jnp.where(me % stride == 0, (me // stride) * n_lk + my_lk, slabs)

    def home(i):
        last_one = i // slabs
        return (
            (1 - last_one) * (i // n_lk) * stride + last_one,
            (1 - last_one) * lax.rem(i, n_lk),
        )

    def to_home(i):
        od, lk = home(i)
        return pltpu.make_async_remote_copy(
            src_ref=sums.at[i], dst_ref=got_s.at[me_all], send_sem=s_send.at[i],
            recv_sem=s_recv.at[me_all], device_id={"od": od, "lk": lk}, device_id_type=MESH,
        )

    def not_mine(action):
        def body(i):
            od, lk = home(i)

            @pl.when((od != me) | (lk != my_lk))
            def _():
                action(i)

        loop(0, slabs + 1, body)

    def from_home(step, i):
        peer = lax.rem(me_all + step, n_all)
        return pltpu.make_async_remote_copy(
            src_ref=full.at[i], dst_ref=full.at[i], send_sem=t_send.at[step],
            recv_sem=t_recv.at[i], device_id=place(peer), device_id_type=MESH,
        )

    def await_part(step):
        peer = lax.rem(me_all + step, n_all)
        pltpu.make_async_remote_copy(
            src_ref=sums.at[0], dst_ref=got_s.at[peer], send_sem=s_send.at[0],
            recv_sem=s_recv.at[peer], device_id=place(peer), device_id_type=MESH,
        ).wait_recv()

    not_mine(lambda i: to_home(i).start())

    @pl.when(summer)
    def _():
        got_s[me_all] = sums[mine]
        loop(1, n_all, await_part)
        full[mine] = jnp.sum(got_s[...], axis=0)
        loop(1, n_all, lambda step: from_home(step, mine).start())

    not_mine(lambda i: from_home(1, i).wait_recv())
    out_ref[...] = full[...]

    def drain(peer):
        push(ask.at[peer], got_ask, ask_send, ask_recv, me, peer).wait_send()
        push(send_m.at[peer], got_m, m_send, m_recv, me, peer).wait_send()
        push(send_f.at[peer], got_f, f_send, f_recv, me, peer).wait_send()

    others(drain, True)
    not_mine(lambda i: to_home(i).wait_send())

    @pl.when(summer)
    def _():
        loop(1, n_all, lambda step: from_home(step, mine).wait_send())


@jax.jit
def inverse_factor(a):
    size = a.shape[0]
    lane = lax.broadcasted_iota(jnp.int32, (1, size), 1)
    sub = lax.broadcasted_iota(jnp.int32, (8, size), 0)
    lanes = lax.broadcasted_iota(jnp.int32, (8, size), 1)
    groups = [a[8 * g:8 * g + 8, :] for g in range(size // 8)]
    for j in range(size):
        at, offset = j // 8, j % 8
        here = lane == j
        row = groups[at][offset:offset + 1, :]
        pivot = jnp.broadcast_to(row[:, j:j + 1], (1, size))
        guess = pl.reciprocal(pivot, approx=True)
        scaled = jnp.where(here, 1.0, row) * (guess * (2.0 - pivot * guess))
        for g in range(at, size // 8):
            if g == at and offset == 7:
                continue
            old = groups[g]
            new = jnp.where(here, 0.0, old) - old[:, j:j + 1] * scaled
            groups[g] = jnp.where(sub > offset, new, old) if g == at else new
    done = []
    for g, rows in enumerate(groups):
        diagonal = lanes == sub + 8 * g
        pivot = jnp.sum(jnp.where(diagonal, rows, 0.0), axis=1, keepdims=True)
        unit = jnp.where(diagonal, 1.0, jnp.where(lanes < sub + 8 * g, rows, 0.0))
        done.append(unit * lax.rsqrt(pivot))
    return jnp.concatenate(done, axis=0)


def update_kernel(start_ref, gram_ref, fac_ref, new_ref, corr_ref, high, low, gain):
    rank = gram_ref.shape[2]
    half = rank // 2
    slabs = half // 8

    @pl.when(pl.program_id(0) == 0)
    def _():
        lane = lax.broadcasted_iota(jnp.int32, (half, half), 1)
        sub = lax.broadcasted_iota(jnp.int32, (half, half), 0)

        packed = gram_ref[0:slabs].reshape(half, rank)
        a21, both = packed[:, :half], packed[:, half:]
        turned = both.T
        extra = gram_ref[slabs]
        a11 = jnp.where(sub >= lane, both, turned) + jnp.where(sub == lane, 1.0, 0.0)
        a22 = jnp.where(sub < lane, both, turned)
        a22 = jnp.where(sub == lane, 1.0 + extra[1:2, :half], a22)
        w1 = inverse_factor(a11)
        l21 = dot(a21, w1, ((1,), (1,)), HIGHEST)
        a22 = a22 - dot(l21, l21, ((1,), (1,)), HIGHEST)
        w2 = inverse_factor(a22)
        w21 = -dot(w2, dot(l21, w1, ((1,), (0,)), HIGHEST), ((1,), (0,)), HIGHEST)
        inverse = jnp.concatenate(
            [jnp.concatenate([w1, jnp.zeros((half, half), jnp.float32)], axis=1),
             jnp.concatenate([w21, w2], axis=1)], axis=0,
        )
        projected = jnp.broadcast_to(extra[0:1, :], (8, rank))
        inner = dot(projected, inverse, ((1,), (1,)), HIGHEST)
        vector = dot(inner, inverse, ((1,), (0,)), HIGHEST)
        top = vector.astype(jnp.bfloat16)
        rest = vector - top.astype(jnp.float32)
        middle = rest.astype(jnp.bfloat16)
        last = (rest - middle.astype(jnp.float32)).astype(jnp.bfloat16)
        gain[...] = jnp.concatenate([top, middle, last], axis=0)
        turned = inverse.T
        upper = turned.astype(jnp.bfloat16)
        high[...] = upper
        low[...] = (turned - upper.astype(jnp.float32)).astype(jnp.bfloat16)

    rows = fac_ref[...]
    new_ref[...] = dot(rows, high[...], ((1,), (0,))) + dot(rows, low[...], ((1,), (0,)))
    parts = dot(gain[...], rows, ((1,), (1,)))
    corr_ref[0] = parts[0:1] + parts[8:9] + parts[16:17]


def per_device(factor, prior_mean, counts, noise_std, owner_ids, local_ids, ecmp, route_share):
    n_od, n_lk = lax.axis_size("od"), lax.axis_size("lk")
    group_tiles, nb = owner_ids.shape
    tiles = group_tiles // n_lk
    link_rows, block_rows = route_share.shape[2:]
    rank = factor.shape[1]
    blocks = factor.shape[0] // block_rows
    vmem = pl.BlockSpec(memory_space=VMEM)
    smem = pl.BlockSpec(memory_space=pltpu.SMEM)
    dma = pltpu.SemaphoreType.DMA

    n_all = n_od * n_lk
    slabs = rank // 16 + 1
    slab = (slabs, 8, rank)
    summed = pl.pallas_call(
        functools.partial(link_kernel, n_od, n_lk, tiles, nb),
        out_shape=jax.ShapeDtypeStruct(slab, jnp.float32),
        in_specs=[smem, smem, smem, vmem, vmem, vmem, vmem, pl.BlockSpec(memory_space=pl.ANY)],
        out_specs=vmem,
        scratch_shapes=[
            VMEM((n_od, 8, 128), jnp.int32),
            VMEM((n_od, 8, 128), jnp.int32),
            pltpu.SMEM((n_od, 8, 128), jnp.int32),
            VMEM((n_od, tiles, block_rows, rank), jnp.bfloat16),
            VMEM((n_od, tiles, block_rows, rank), jnp.bfloat16),
            VMEM((n_od, 8, block_rows), jnp.float32),
            VMEM((n_od, 8, block_rows), jnp.float32),
            VMEM((tiles, nb, link_rows, block_rows), jnp.bfloat16),
            VMEM((tiles, link_rows, rank), jnp.float32),
            VMEM((tiles, 8, link_rows), jnp.float32),
            VMEM(slab, jnp.float32),
            VMEM((n_all, 8, rank), jnp.float32),
            VMEM(slab, jnp.float32),
        ] + [dma((n_od,))] * 6 + [dma((slabs,)), dma((n_all,)), dma((n_all,)), dma((slabs,))]
        + [dma, dma],
        compiler_params=pltpu.CompilerParams(
            collective_id=0, has_side_effects=True, vmem_limit_bytes=56 * 1024 * 1024
        ),
        name="links",
    )(
        owner_ids, local_ids, ecmp,
        prior_mean.astype(jnp.float32).reshape(blocks, 1, block_rows),
        counts.reshape(tiles, link_rows), noise_std.reshape(tiles, link_rows),
        factor.reshape(blocks, block_rows, rank), route_share,
    )

    own_rows = factor.shape[0] // n_lk
    step_rows = min(512, own_rows)
    steps = own_rows // step_rows
    start = (lax.axis_index("lk") * steps).astype(jnp.int32).reshape(1)
    new_factor, correction = pl.pallas_call(
        update_kernel,
        out_shape=(
            jax.ShapeDtypeStruct((own_rows, rank), jnp.float32),
            jax.ShapeDtypeStruct((steps, 1, step_rows), jnp.float32),
        ),
        grid_spec=pltpu.PrefetchScalarGridSpec(
            num_scalar_prefetch=1,
            grid=(steps,),
            in_specs=[
                pl.BlockSpec(slab, lambda i, start: (0, 0, 0)),
                pl.BlockSpec((step_rows, rank), lambda i, start: (start[0] + i, 0)),
            ],
            out_specs=[
                pl.BlockSpec((step_rows, rank), lambda i, start: (i, 0)),
                pl.BlockSpec((1, 1, step_rows), lambda i, start: (i, 0, 0)),
            ],
            scratch_shapes=[
                VMEM((rank, rank), jnp.bfloat16),
                VMEM((rank, rank), jnp.bfloat16),
                VMEM((24, rank), jnp.bfloat16),
            ],
        ),
        compiler_params=pltpu.CompilerParams(vmem_limit_bytes=32 * 1024 * 1024),
        name="update",
    )(start, summed, factor)
    return (new_factor, correction.reshape(-1))


def solution(mesh):
    in_specs = (
        P("od", None),
        P("od"),
        P(("od", "lk")),
        P(("od", "lk")),
        P("od", None),
        P("od", None),
        P("od", None),
        P("od", None, None, None),
    )
    out_specs = (P(("od", "lk"), None), P(("od", "lk")))
    return jax.shard_map(
        per_device, mesh=mesh, in_specs=in_specs, out_specs=out_specs, check_vma=False
    )
```

```python
import functools

import jax
import jax.numpy as jnp
from jax import lax
from jax.experimental import pallas as pl
from jax.experimental.pallas import tpu as pltpu
from jax.sharding import PartitionSpec as P

MESH = pl.DeviceIdType.MESH
HIGHEST = lax.Precision.HIGHEST
VMEM = pltpu.VMEM


def dot(a, b, contract, precision=None):
    return lax.dot_general(
        a, b, (contract, ((), ())), precision=precision, preferred_element_type=jnp.float32
    )


def split(a):
    high = a.astype(jnp.bfloat16)
    return high, (a - high.astype(jnp.float32)).astype(jnp.bfloat16)


def link_kernel(
    n, n_lk, tiles, nb, owner_ref, local_ref, ecmp_ref, mean_ref, counts_ref, std_ref,
    fac_ref, route_hbm, out_ref,
    ask, got_ask, ask_smem, send_f, got_f, send_m, got_m, route, linked, predicted,
    sums, got_s, full,
    ask_send, ask_recv, f_send, f_recv, m_send, m_recv, s_send, s_recv, t_send, t_recv,
    local_sem, route_sem,
):
    me, my_lk = lax.axis_index("od"), lax.axis_index("lk")
    first = my_lk * tiles
    rank = fac_ref.shape[2]
    n_all = n * n_lk
    me_all = me * n_lk + my_lk
    half = n // 2

    load_route = pltpu.make_async_copy(route_hbm.at[pl.ds(first, tiles)], route, route_sem)
    load_route.start()

    barrier = pltpu.get_barrier_semaphore()

    def loop(start, stop, action):
        def body(step, carry):
            action(step)
            return carry

        lax.fori_loop(start, stop, body, 0)

    def place(index):
        return {"od": index // n_lk, "lk": lax.rem(index, n_lk)}

    def greet(step):
        where = place(lax.rem(me_all + step, n_all))
        pl.semaphore_signal(barrier, inc=1, device_id=where, device_id_type=MESH)

    loop(1, n_all, greet)

    owner_iota = lax.broadcasted_iota(jnp.int32, ask.shape, 0)
    lane = lax.broadcasted_iota(jnp.int32, ask.shape, 2)
    table = jnp.zeros(ask.shape, jnp.int32)
    for t in range(tiles):
        for k in range(nb):
            hit = (owner_iota == owner_ref[first + t, k]) & (lane == t)
            table = jnp.where(hit, local_ref[first + t, k], table)
    ask[...] = table
    send_m[...] = jnp.zeros_like(send_m)
    linked[...] = jnp.zeros_like(linked)
    predicted[...] = jnp.zeros_like(predicted)
    pl.semaphore_wait(barrier, n_all - 1)

    def push(src, dst, send_sem, recv_sem, at, peer):
        return pltpu.make_async_remote_copy(
            src_ref=src, dst_ref=dst.at[at], send_sem=send_sem.at[peer],
            recv_sem=recv_sem.at[at], device_id={"od": peer}, device_id_type=MESH,
        )

    def far(step):
        return (1 - me // half) * half + lax.rem(me + step, half)

    def near(step):
        return (me // half) * half + lax.rem(me + step, half)

    def others(action, far_first):
        if far_first:
            loop(0, half, lambda step: action(far(step)))
        loop(1, half, lambda step: action(near(step)))
        if not far_first:
            loop(0, half, lambda step: action(far(step)))

    others(lambda peer: push(ask.at[peer], got_ask, ask_send, ask_recv, me, peer).start(), True)
    got_ask[me] = ask[me]
    others(
        lambda peer: push(ask.at[peer], got_ask, ask_send, ask_recv, peer, peer).wait_recv(), False
    )
    to_smem = pltpu.make_async_copy(got_ask, ask_smem, local_sem)
    to_smem.start()
    to_smem.wait()

    def serve(t, peer):
        index = ask_smem[peer, 0, t]
        send_f[peer, t] = fac_ref[index]
        send_m[peer, t:t + 1] = mean_ref[index]
        push(send_f.at[peer, t], got_f.at[:, t], f_send, f_recv, me, peer).start()

    for t in range(tiles):
        loop(1, n, lambda step, t=t: serve(t, lax.rem(me + step, n)))
    others(lambda peer: push(send_m.at[peer], got_m, m_send, m_recv, me, peer).start(), True)
    got_m[me] = jnp.zeros(send_m.shape[1:], jnp.float32)
    for t in range(tiles):
        index = ask_smem[me, 0, t]
        got_f[me, t] = fac_ref[index]
        got_m[me, t:t + 1] = mean_ref[index]
    spread = [jnp.broadcast_to(std_ref[t:t + 1, :], (128, 128)).T for t in range(tiles)]
    load_route.wait()

    def use(owner):
        means = got_m[owner].astype(jnp.bfloat16)
        for t in range(tiles):
            slot, times = 0, 0
            for k in range(nb):
                named = owner_ref[first + t, k] == owner
                slot = jnp.where(named, k, slot)
                times = jnp.where(named, ecmp_ref[first + t, k], times)
            times = times.astype(jnp.float32)
            share = route[t, slot]
            linked[t] += times * dot(share, got_f[owner, t], ((1,), (0,)))
            predicted[t] += times * dot(means, share, ((1,), (1,)))

    def arrive(peer):
        push(send_m.at[peer], got_m, m_send, m_recv, peer, peer).wait_recv()
        push(send_f.at[peer], got_f, f_send, f_recv, peer, peer).wait_recv()
        use(peer)

    use(me)
    others(arrive, False)

    whole, innovation = [], []
    for t in range(tiles):
        whole.append(linked[t] / jnp.concatenate([spread[t]] * (rank // 128), axis=1))
        innovation.append(
            (counts_ref[t:t + 1, :] - predicted[t, t:t + 1, :]) / std_ref[t:t + 1, :]
        )
    high, low = split(jnp.concatenate(whole, axis=0))
    in_high, in_low = split(jnp.broadcast_to(
        jnp.concatenate(innovation, axis=1), (8, tiles * 128)
    ))
    cross = dot(high, low, ((0,), (0,)))
    gram = dot(high, high, ((0,), (0,))) + (cross + cross.T)
    projected = dot(in_high, high, ((1,), (0,))) + (
        dot(in_low, high, ((1,), (0,))) + dot(in_high, low, ((1,), (0,)))
    )
    mid = rank // 2
    row = lax.broadcasted_iota(jnp.int32, (mid, mid), 0)
    column = lax.broadcasted_iota(jnp.int32, (mid, mid), 1)
    last = gram[mid:, mid:]
    slabs = mid // 8
    sums[0:slabs, :, :mid] = gram[mid:, :mid].reshape(slabs, 8, mid)
    sums[0:slabs, :, mid:] = jnp.where(row >= column, gram[:mid, :mid], last).reshape(
        slabs, 8, mid
    )
    diagonal = jnp.sum(jnp.where(row == column, last, 0.0), axis=0, keepdims=True)
    diagonal = jnp.concatenate([diagonal, diagonal], axis=1)
    eight = lax.broadcasted_iota(jnp.int32, (8, rank), 0)
    sums[slabs] = jnp.where(eight == 0, projected, diagonal)

    stride = n_all // slabs
    summer = (me % stride == 0) | ((me == 1) & (my_lk == 0))
    mine = jnp.where(me % stride == 0, (me // stride) * n_lk + my_lk, slabs)

    def home(i):
        last_one = i // slabs
        return (
            (1 - last_one) * (i // n_lk) * stride + last_one,
            (1 - last_one) * lax.rem(i, n_lk),
        )

    def to_home(i):
        od, lk = home(i)
        return pltpu.make_async_remote_copy(
            src_ref=sums.at[i], dst_ref=got_s.at[me_all], send_sem=s_send.at[i],
            recv_sem=s_recv.at[me_all], device_id={"od": od, "lk": lk}, device_id_type=MESH,
        )

    def not_mine(action):
        def body(i):
            od, lk = home(i)

            @pl.when((od != me) | (lk != my_lk))
            def _():
                action(i)

        loop(0, slabs + 1, body)

    def from_home(step, i):
        peer = lax.rem(me_all + step, n_all)
        return pltpu.make_async_remote_copy(
            src_ref=full.at[i], dst_ref=full.at[i], send_sem=t_send.at[step],
            recv_sem=t_recv.at[i], device_id=place(peer), device_id_type=MESH,
        )

    def await_part(step):
        peer = lax.rem(me_all + step, n_all)
        pltpu.make_async_remote_copy(
            src_ref=sums.at[0], dst_ref=got_s.at[peer], send_sem=s_send.at[0],
            recv_sem=s_recv.at[peer], device_id=place(peer), device_id_type=MESH,
        ).wait_recv()

    not_mine(lambda i: to_home(i).start())

    @pl.when(summer)
    def _():
        got_s[me_all] = sums[mine]
        loop(1, n_all, await_part)
        full[mine] = jnp.sum(got_s[...], axis=0)
        loop(1, n_all, lambda step: from_home(step, mine).start())

    not_mine(lambda i: from_home(1, i).wait_recv())
    out_ref[...] = full[...]

    def drain(peer):
        push(ask.at[peer], got_ask, ask_send, ask_recv, me, peer).wait_send()
        push(send_m.at[peer], got_m, m_send, m_recv, me, peer).wait_send()
        push(send_f.at[peer], got_f, f_send, f_recv, me, peer).wait_send()

    others(drain, True)
    not_mine(lambda i: to_home(i).wait_send())

    @pl.when(summer)
    def _():
        loop(1, n_all, lambda step: from_home(step, mine).wait_send())


@jax.jit
def inverse_factor(a):
    size = a.shape[0]
    lane = lax.broadcasted_iota(jnp.int32, (1, size), 1)
    sub = lax.broadcasted_iota(jnp.int32, (8, size), 0)
    lanes = lax.broadcasted_iota(jnp.int32, (8, size), 1)
    groups = [a[8 * g:8 * g + 8, :] for g in range(size // 8)]
    for j in range(size):
        at, offset = j // 8, j % 8
        here = lane == j
        row = groups[at][offset:offset + 1, :]
        scaled = jnp.where(here, 1.0, row) / row[:, j:j + 1]
        for g in range(at, size // 8):
            if g == at and offset == 7:
                continue
            old = groups[g]
            new = jnp.where(here, 0.0, old) - old[:, j:j + 1] * scaled
            groups[g] = jnp.where(sub > offset, new, old) if g == at else new
    done = []
    for g, rows in enumerate(groups):
        diagonal = lanes == sub + 8 * g
        pivot = jnp.sum(jnp.where(diagonal, rows, 0.0), axis=1, keepdims=True)
        unit = jnp.where(diagonal, 1.0, jnp.where(lanes < sub + 8 * g, rows, 0.0))
        done.append(unit * lax.rsqrt(pivot))
    return jnp.concatenate(done, axis=0)


def update_kernel(start_ref, gram_ref, fac_ref, new_ref, corr_ref, high, low, gain):
    rank = gram_ref.shape[2]
    half = rank // 2
    slabs = half // 8

    @pl.when(pl.program_id(0) == 0)
    def _():
        lane = lax.broadcasted_iota(jnp.int32, (half, half), 1)
        sub = lax.broadcasted_iota(jnp.int32, (half, half), 0)

        packed = gram_ref[0:slabs].reshape(half, rank)
        a21, both = packed[:, :half], packed[:, half:]
        turned = both.T
        extra = gram_ref[slabs]
        a11 = jnp.where(sub >= lane, both, turned) + jnp.where(sub == lane, 1.0, 0.0)
        a22 = jnp.where(sub < lane, both, turned)
        a22 = jnp.where(sub == lane, 1.0 + extra[1:2, :half], a22)
        w1 = inverse_factor(a11)
        l21 = dot(a21, w1, ((1,), (1,)), HIGHEST)
        a22 = a22 - dot(l21, l21, ((1,), (1,)), HIGHEST)
        w2 = inverse_factor(a22)
        w21 = -dot(w2, dot(l21, w1, ((1,), (0,)), HIGHEST), ((1,), (0,)), HIGHEST)
        inverse = jnp.concatenate(
            [jnp.concatenate([w1, jnp.zeros((half, half), jnp.float32)], axis=1),
             jnp.concatenate([w21, w2], axis=1)], axis=0,
        )
        projected = jnp.broadcast_to(extra[0:1, :], (8, rank))
        inner = dot(projected, inverse, ((1,), (1,)), HIGHEST)
        vector = dot(inner, inverse, ((1,), (0,)), HIGHEST)
        top = vector.astype(jnp.bfloat16)
        rest = vector - top.astype(jnp.float32)
        middle = rest.astype(jnp.bfloat16)
        last = (rest - middle.astype(jnp.float32)).astype(jnp.bfloat16)
        gain[...] = jnp.concatenate([top, middle, last], axis=0)
        turned = inverse.T
        upper = turned.astype(jnp.bfloat16)
        high[...] = upper
        low[...] = (turned - upper.astype(jnp.float32)).astype(jnp.bfloat16)

    rows = fac_ref[...]
    new_ref[...] = dot(rows, high[...], ((1,), (0,))) + dot(rows, low[...], ((1,), (0,)))
    parts = dot(gain[...], rows, ((1,), (1,)))
    corr_ref[0] = parts[0:1] + parts[8:9] + parts[16:17]


def per_device(factor, prior_mean, counts, noise_std, owner_ids, local_ids, ecmp, route_share):
    n_od, n_lk = lax.axis_size("od"), lax.axis_size("lk")
    group_tiles, nb = owner_ids.shape
    tiles = group_tiles // n_lk
    link_rows, block_rows = route_share.shape[2:]
    rank = factor.shape[1]
    blocks = factor.shape[0] // block_rows
    vmem = pl.BlockSpec(memory_space=VMEM)
    smem = pl.BlockSpec(memory_space=pltpu.SMEM)
    dma = pltpu.SemaphoreType.DMA

    n_all = n_od * n_lk
    slabs = rank // 16 + 1
    slab = (slabs, 8, rank)
    summed = pl.pallas_call(
        functools.partial(link_kernel, n_od, n_lk, tiles, nb),
        out_shape=jax.ShapeDtypeStruct(slab, jnp.float32),
        in_specs=[smem, smem, smem, vmem, vmem, vmem, vmem, pl.BlockSpec(memory_space=pl.ANY)],
        out_specs=vmem,
        scratch_shapes=[
            VMEM((n_od, 8, 128), jnp.int32),
            VMEM((n_od, 8, 128), jnp.int32),
            pltpu.SMEM((n_od, 8, 128), jnp.int32),
            VMEM((n_od, tiles, block_rows, rank), jnp.bfloat16),
            VMEM((n_od, tiles, block_rows, rank), jnp.bfloat16),
            VMEM((n_od, 8, block_rows), jnp.float32),
            VMEM((n_od, 8, block_rows), jnp.float32),
            VMEM((tiles, nb, link_rows, block_rows), jnp.bfloat16),
            VMEM((tiles, link_rows, rank), jnp.float32),
            VMEM((tiles, 8, link_rows), jnp.float32),
            VMEM(slab, jnp.float32),
            VMEM((n_all, 8, rank), jnp.float32),
            VMEM(slab, jnp.float32),
        ] + [dma((n_od,))] * 6 + [dma((slabs,)), dma((n_all,)), dma((n_all,)), dma((slabs,))]
        + [dma, dma],
        compiler_params=pltpu.CompilerParams(
            collective_id=0, has_side_effects=True, vmem_limit_bytes=56 * 1024 * 1024
        ),
        name="links",
    )(
        owner_ids, local_ids, ecmp,
        prior_mean.astype(jnp.float32).reshape(blocks, 1, block_rows),
        counts.reshape(tiles, link_rows), noise_std.reshape(tiles, link_rows),
        factor.reshape(blocks, block_rows, rank), route_share,
    )

    own_rows = factor.shape[0] // n_lk
    step_rows = min(512, own_rows)
    steps = own_rows // step_rows
    start = (lax.axis_index("lk") * steps).astype(jnp.int32).reshape(1)
    new_factor, correction = pl.pallas_call(
        update_kernel,
        out_shape=(
            jax.ShapeDtypeStruct((own_rows, rank), jnp.float32),
            jax.ShapeDtypeStruct((steps, 1, step_rows), jnp.float32),
        ),
        grid_spec=pltpu.PrefetchScalarGridSpec(
            num_scalar_prefetch=1,
            grid=(steps,),
            in_specs=[
                pl.BlockSpec(slab, lambda i, start: (0, 0, 0)),
                pl.BlockSpec((step_rows, rank), lambda i, start: (start[0] + i, 0)),
            ],
            out_specs=[
                pl.BlockSpec((step_rows, rank), lambda i, start: (i, 0)),
                pl.BlockSpec((1, 1, step_rows), lambda i, start: (i, 0, 0)),
            ],
            scratch_shapes=[
                VMEM((rank, rank), jnp.bfloat16),
                VMEM((rank, rank), jnp.bfloat16),
                VMEM((24, rank), jnp.bfloat16),
            ],
        ),
        compiler_params=pltpu.CompilerParams(vmem_limit_bytes=32 * 1024 * 1024),
        name="update",
    )(start, summed, factor)
    return (new_factor, correction.reshape(-1))


def solution(mesh):
    in_specs = (
        P("od", None),
        P("od"),
        P(("od", "lk")),
        P(("od", "lk")),
        P("od", None),
        P("od", None),
        P("od", None),
        P("od", None, None, None),
    )
    out_specs = (P(("od", "lk"), None), P(("od", "lk")))
    return jax.shard_map(
        per_device, mesh=mesh, in_specs=in_specs, out_specs=out_specs, check_vma=False
    )
```

```python
import functools

import jax
import jax.numpy as jnp
from jax import lax
from jax.experimental import pallas as pl
from jax.experimental.pallas import tpu as pltpu
from jax.sharding import PartitionSpec as P

MESH = pl.DeviceIdType.MESH
HIGHEST = lax.Precision.HIGHEST
VMEM = pltpu.VMEM


def dot(a, b, contract, precision=None):
    return lax.dot_general(
        a, b, (contract, ((), ())), precision=precision, preferred_element_type=jnp.float32
    )


def split(a):
    high = a.astype(jnp.bfloat16)
    return high, (a - high.astype(jnp.float32)).astype(jnp.bfloat16)


def link_kernel(
    n, n_lk, tiles, nb, owner_ref, local_ref, ecmp_ref, mean_ref, counts_ref, std_ref,
    fac_ref, route_hbm, out_ref,
    ask, got_ask, ask_smem, send_f, got_f, send_m, got_m, route, linked, predicted,
    sums, got_s, full,
    ask_send, ask_recv, f_send, f_recv, m_send, m_recv, s_send, s_recv, t_send, t_recv,
    local_sem, route_sem,
):
    me, my_lk = lax.axis_index("od"), lax.axis_index("lk")
    first = my_lk * tiles
    rank = fac_ref.shape[2]
    n_all = n * n_lk
    me_all = me * n_lk + my_lk
    half = n // 2

    load_route = pltpu.make_async_copy(route_hbm.at[pl.ds(first, tiles)], route, route_sem)
    load_route.start()

    barrier = pltpu.get_barrier_semaphore()

    def loop(start, stop, action):
        def body(step, carry):
            action(step)
            return carry

        lax.fori_loop(start, stop, body, 0)

    def place(index):
        return {"od": index // n_lk, "lk": lax.rem(index, n_lk)}

    def greet(step):
        where = place(lax.rem(me_all + step, n_all))
        pl.semaphore_signal(barrier, inc=1, device_id=where, device_id_type=MESH)

    loop(1, n_all, greet)

    owner_iota = lax.broadcasted_iota(jnp.int32, ask.shape, 0)
    lane = lax.broadcasted_iota(jnp.int32, ask.shape, 2)
    table = jnp.zeros(ask.shape, jnp.int32)
    for t in range(tiles):
        for k in range(nb):
            hit = (owner_iota == owner_ref[first + t, k]) & (lane == t)
            table = jnp.where(hit, local_ref[first + t, k], table)
    ask[...] = table
    send_m[...] = jnp.zeros_like(send_m)
    linked[...] = jnp.zeros_like(linked)
    predicted[...] = jnp.zeros_like(predicted)
    pl.semaphore_wait(barrier, n_all - 1)

    def push(src, dst, send_sem, recv_sem, at, peer):
        return pltpu.make_async_remote_copy(
            src_ref=src, dst_ref=dst.at[at], send_sem=send_sem.at[peer],
            recv_sem=recv_sem.at[at], device_id={"od": peer}, device_id_type=MESH,
        )

    def far(step):
        return (1 - me // half) * half + lax.rem(me + step, half)

    def near(step):
        return (me // half) * half + lax.rem(me + step, half)

    def others(action, far_first):
        if far_first:
            loop(0, half, lambda step: action(far(step)))
        loop(1, half, lambda step: action(near(step)))
        if not far_first:
            loop(0, half, lambda step: action(far(step)))

    others(lambda peer: push(ask.at[peer], got_ask, ask_send, ask_recv, me, peer).start(), True)
    got_ask[me] = ask[me]
    others(
        lambda peer: push(ask.at[peer], got_ask, ask_send, ask_recv, peer, peer).wait_recv(), False
    )
    to_smem = pltpu.make_async_copy(got_ask, ask_smem, local_sem)
    to_smem.start()
    to_smem.wait()

    def serve(t, peer):
        index = ask_smem[peer, 0, t]
        send_f[peer, t] = fac_ref[index]
        send_m[peer, t:t + 1] = mean_ref[index]
        push(send_f.at[peer, t], got_f.at[:, t], f_send, f_recv, me, peer).start()

    for t in range(tiles):
        loop(1, n, lambda step, t=t: serve(t, lax.rem(me + step, n)))
    others(lambda peer: push(send_m.at[peer], got_m, m_send, m_recv, me, peer).start(), True)
    got_m[me] = jnp.zeros(send_m.shape[1:], jnp.float32)
    for t in range(tiles):
        index = ask_smem[me, 0, t]
        got_f[me, t] = fac_ref[index]
        got_m[me, t:t + 1] = mean_ref[index]
    spread = [jnp.broadcast_to(std_ref[t:t + 1, :], (128, 128)).T for t in range(tiles)]
    load_route.wait()

    def use(owner):
        means = got_m[owner].astype(jnp.bfloat16)
        for t in range(tiles):
            slot, times = 0, 0
            for k in range(nb):
                named = owner_ref[first + t, k] == owner
                slot = jnp.where(named, k, slot)
                times = jnp.where(named, ecmp_ref[first + t, k], times)
            times = times.astype(jnp.float32)
            share = route[t, slot]
            linked[t] += times * dot(share, got_f[owner, t], ((1,), (0,)))
            predicted[t] += times * dot(means, share, ((1,), (1,)))

    def arrive(peer):
        push(send_m.at[peer], got_m, m_send, m_recv, peer, peer).wait_recv()
        push(send_f.at[peer], got_f, f_send, f_recv, peer, peer).wait_recv()
        use(peer)

    use(me)
    others(arrive, False)

    whole, innovation = [], []
    for t in range(tiles):
        whole.append(linked[t] / jnp.concatenate([spread[t]] * (rank // 128), axis=1))
        innovation.append(
            (counts_ref[t:t + 1, :] - predicted[t, t:t + 1, :]) / std_ref[t:t + 1, :]
        )
    high, low = split(jnp.concatenate(whole, axis=0))
    in_high, in_low = split(jnp.broadcast_to(
        jnp.concatenate(innovation, axis=1), (8, tiles * 128)
    ))
    cross = dot(high, low, ((0,), (0,)))
    gram = dot(high, high, ((0,), (0,))) + (cross + cross.T)
    projected = dot(in_high, high, ((1,), (0,))) + (
        dot(in_low, high, ((1,), (0,))) + dot(in_high, low, ((1,), (0,)))
    )
    mid = rank // 2
    row = lax.broadcasted_iota(jnp.int32, (mid, mid), 0)
    column = lax.broadcasted_iota(jnp.int32, (mid, mid), 1)
    last = gram[mid:, mid:]
    slabs = mid // 8
    sums[0:slabs, :, :mid] = gram[mid:, :mid].reshape(slabs, 8, mid)
    sums[0:slabs, :, mid:] = jnp.where(row >= column, gram[:mid, :mid], last).reshape(
        slabs, 8, mid
    )
    diagonal = jnp.sum(jnp.where(row == column, last, 0.0), axis=0, keepdims=True)
    diagonal = jnp.concatenate([diagonal, diagonal], axis=1)
    eight = lax.broadcasted_iota(jnp.int32, (8, rank), 0)
    sums[slabs] = jnp.where(eight == 0, projected, diagonal)

    stride = n_all // slabs
    summer = (me % stride == 0) | ((me == 1) & (my_lk == 0))
    mine = jnp.where(me % stride == 0, (me // stride) * n_lk + my_lk, slabs)

    def home(i):
        last_one = i // slabs
        return (
            (1 - last_one) * (i // n_lk) * stride + last_one,
            (1 - last_one) * lax.rem(i, n_lk),
        )

    def to_home(i):
        od, lk = home(i)
        return pltpu.make_async_remote_copy(
            src_ref=sums.at[i], dst_ref=got_s.at[me_all], send_sem=s_send.at[i],
            recv_sem=s_recv.at[me_all], device_id={"od": od, "lk": lk}, device_id_type=MESH,
        )

    def not_mine(action):
        def body(i):
            od, lk = home(i)

            @pl.when((od != me) | (lk != my_lk))
            def _():
                action(i)

        loop(0, slabs + 1, body)

    def from_home(step, i):
        peer = lax.rem(me_all + step, n_all)
        return pltpu.make_async_remote_copy(
            src_ref=full.at[i], dst_ref=full.at[i], send_sem=t_send.at[step],
            recv_sem=t_recv.at[i], device_id=place(peer), device_id_type=MESH,
        )

    def await_part(step):
        peer = lax.rem(me_all + step, n_all)
        pltpu.make_async_remote_copy(
            src_ref=sums.at[0], dst_ref=got_s.at[peer], send_sem=s_send.at[0],
            recv_sem=s_recv.at[peer], device_id=place(peer), device_id_type=MESH,
        ).wait_recv()

    not_mine(lambda i: to_home(i).start())

    @pl.when(summer)
    def _():
        got_s[me_all] = sums[mine]
        loop(1, n_all, await_part)
        full[mine] = jnp.sum(got_s[...], axis=0)
        loop(1, n_all, lambda step: from_home(step, mine).start())

    not_mine(lambda i: from_home(1, i).wait_recv())
    out_ref[...] = full[...]

    def drain(peer):
        push(ask.at[peer], got_ask, ask_send, ask_recv, me, peer).wait_send()
        push(send_m.at[peer], got_m, m_send, m_recv, me, peer).wait_send()
        push(send_f.at[peer], got_f, f_send, f_recv, me, peer).wait_send()

    others(drain, True)
    not_mine(lambda i: to_home(i).wait_send())

    @pl.when(summer)
    def _():
        loop(1, n_all, lambda step: from_home(step, mine).wait_send())


@jax.jit
def inverse_factor(a):
    size = a.shape[0]
    lane = lax.broadcasted_iota(jnp.int32, (1, size), 1)
    sub = lax.broadcasted_iota(jnp.int32, (8, size), 0)
    lanes = lax.broadcasted_iota(jnp.int32, (8, size), 1)
    groups = [a[8 * g:8 * g + 8, :] for g in range(size // 8)]
    for j in range(size):
        at, offset = j // 8, j % 8
        here = lane == j
        row = groups[at][offset:offset + 1, :]
        scaled = jnp.where(here, 1.0, row) / row[:, j:j + 1]
        for g in range(at, size // 8):
            if g == at and offset == 7:
                continue
            old = groups[g]
            new = jnp.where(here, 0.0, old) - old[:, j:j + 1] * scaled
            groups[g] = jnp.where(sub > offset, new, old) if g == at else new
    done = []
    for g, rows in enumerate(groups):
        diagonal = lanes == sub + 8 * g
        pivot = jnp.sum(jnp.where(diagonal, rows, 0.0), axis=1, keepdims=True)
        unit = jnp.where(diagonal, 1.0, jnp.where(lanes < sub + 8 * g, rows, 0.0))
        done.append(unit * lax.rsqrt(pivot))
    return jnp.concatenate(done, axis=0)


def update_kernel(start_ref, gram_ref, fac_ref, new_ref, corr_ref, high, low, gain):
    rank = gram_ref.shape[2]
    half = rank // 2
    slabs = half // 8

    @pl.when(pl.program_id(0) == 0)
    def _():
        lane = lax.broadcasted_iota(jnp.int32, (half, half), 1)
        sub = lax.broadcasted_iota(jnp.int32, (half, half), 0)

        packed = gram_ref[0:slabs].reshape(half, rank)
        a21, both = packed[:, :half], packed[:, half:]
        turned = both.T
        extra = gram_ref[slabs]
        a11 = jnp.where(sub >= lane, both, turned) + jnp.where(sub == lane, 1.0, 0.0)
        a22 = jnp.where(sub < lane, both, turned)
        a22 = jnp.where(sub == lane, 1.0 + extra[1:2, :half], a22)
        w1 = inverse_factor(a11)
        l21 = dot(a21, w1, ((1,), (1,)), HIGHEST)
        a22 = a22 - dot(l21, l21, ((1,), (1,)), HIGHEST)
        w2 = inverse_factor(a22)
        w21 = -dot(w2, dot(l21, w1, ((1,), (0,)), HIGHEST), ((1,), (0,)), HIGHEST)
        inverse = jnp.concatenate(
            [jnp.concatenate([w1, jnp.zeros((half, half), jnp.float32)], axis=1),
             jnp.concatenate([w21, w2], axis=1)], axis=0,
        )
        projected = jnp.broadcast_to(extra[0:1, :], (8, rank))
        inner = dot(projected, inverse, ((1,), (1,)), HIGHEST)
        vector = dot(inner, inverse, ((1,), (0,)), HIGHEST)
        top = vector.astype(jnp.bfloat16)
        rest = vector - top.astype(jnp.float32)
        middle = rest.astype(jnp.bfloat16)
        last = (rest - middle.astype(jnp.float32)).astype(jnp.bfloat16)
        gain[...] = jnp.concatenate([top, middle, last], axis=0)
        turned = inverse.T
        upper = turned.astype(jnp.bfloat16)
        high[...] = upper
        low[...] = (turned - upper.astype(jnp.float32)).astype(jnp.bfloat16)

    rows = fac_ref[...]
    new_ref[...] = dot(rows, high[...], ((1,), (0,))) + dot(rows, low[...], ((1,), (0,)))
    parts = dot(gain[...], rows, ((1,), (1,)))
    corr_ref[0] = parts[0:1] + parts[8:9] + parts[16:17]


def per_device(factor, prior_mean, counts, noise_std, owner_ids, local_ids, ecmp, route_share):
    n_od, n_lk = lax.axis_size("od"), lax.axis_size("lk")
    group_tiles, nb = owner_ids.shape
    tiles = group_tiles // n_lk
    link_rows, block_rows = route_share.shape[2:]
    rank = factor.shape[1]
    blocks = factor.shape[0] // block_rows
    vmem = pl.BlockSpec(memory_space=VMEM)
    smem = pl.BlockSpec(memory_space=pltpu.SMEM)
    dma = pltpu.SemaphoreType.DMA

    n_all = n_od * n_lk
    slabs = rank // 16 + 1
    slab = (slabs, 8, rank)
    summed = pl.pallas_call(
        functools.partial(link_kernel, n_od, n_lk, tiles, nb),
        out_shape=jax.ShapeDtypeStruct(slab, jnp.float32),
        in_specs=[smem, smem, smem, vmem, vmem, vmem, vmem, pl.BlockSpec(memory_space=pl.ANY)],
        out_specs=vmem,
        scratch_shapes=[
            VMEM((n_od, 8, 128), jnp.int32),
            VMEM((n_od, 8, 128), jnp.int32),
            pltpu.SMEM((n_od, 8, 128), jnp.int32),
            VMEM((n_od, tiles, block_rows, rank), jnp.bfloat16),
            VMEM((n_od, tiles, block_rows, rank), jnp.bfloat16),
            VMEM((n_od, 8, block_rows), jnp.float32),
            VMEM((n_od, 8, block_rows), jnp.float32),
            VMEM((tiles, nb, link_rows, block_rows), jnp.bfloat16),
            VMEM((tiles, link_rows, rank), jnp.float32),
            VMEM((tiles, 8, link_rows), jnp.float32),
            VMEM(slab, jnp.float32),
            VMEM((n_all, 8, rank), jnp.float32),
            VMEM(slab, jnp.float32),
        ] + [dma((n_od,))] * 6 + [dma((slabs,)), dma((n_all,)), dma((n_all,)), dma((slabs,))]
        + [dma, dma],
        compiler_params=pltpu.CompilerParams(
            collective_id=0, has_side_effects=True, vmem_limit_bytes=56 * 1024 * 1024
        ),
        name="links",
    )(
        owner_ids, local_ids, ecmp,
        prior_mean.astype(jnp.float32).reshape(blocks, 1, block_rows),
        counts.reshape(tiles, link_rows), noise_std.reshape(tiles, link_rows),
        factor.reshape(blocks, block_rows, rank), route_share,
    )

    own_rows = factor.shape[0] // n_lk
    step_rows = min(1024, own_rows)
    steps = own_rows // step_rows
    start = (lax.axis_index("lk") * steps).astype(jnp.int32).reshape(1)
    new_factor, correction = pl.pallas_call(
        update_kernel,
        out_shape=(
            jax.ShapeDtypeStruct((own_rows, rank), jnp.float32),
            jax.ShapeDtypeStruct((steps, 1, step_rows), jnp.float32),
        ),
        grid_spec=pltpu.PrefetchScalarGridSpec(
            num_scalar_prefetch=1,
            grid=(steps,),
            in_specs=[
                pl.BlockSpec(slab, lambda i, start: (0, 0, 0)),
                pl.BlockSpec((step_rows, rank), lambda i, start: (start[0] + i, 0)),
            ],
            out_specs=[
                pl.BlockSpec((step_rows, rank), lambda i, start: (i, 0)),
                pl.BlockSpec((1, 1, step_rows), lambda i, start: (i, 0, 0)),
            ],
            scratch_shapes=[
                VMEM((rank, rank), jnp.bfloat16),
                VMEM((rank, rank), jnp.bfloat16),
                VMEM((24, rank), jnp.bfloat16),
            ],
        ),
        compiler_params=pltpu.CompilerParams(vmem_limit_bytes=32 * 1024 * 1024),
        name="update",
    )(start, summed, factor)
    return (new_factor, correction.reshape(-1))


def solution(mesh):
    in_specs = (
        P("od", None),
        P("od"),
        P(("od", "lk")),
        P(("od", "lk")),
        P("od", None),
        P("od", None),
        P("od", None),
        P("od", None, None, None),
    )
    out_specs = (P(("od", "lk"), None), P(("od", "lk")))
    return jax.shard_map(
        per_device, mesh=mesh, in_specs=in_specs, out_specs=out_specs, check_vma=False
    )
```
